32 devices in a mesh: groups: 2 (over x), dp: 16 (over z, y, core).
Axes of the slice: x: 2, y: 2, z: 4, core: 2. Of those that a mesh axis runs over, the one named last changes fastest.
Arguments:
- x_input: bfloat16 [4096, 8192], P(('groups', 'dp')), parts along dimension 0, may hold values from -6 to 6
- bc_input: bfloat16 [4096, 1024], P(('groups', 'dp')), parts along dimension 0, may hold values from -3 to 3
- dt_input: bfloat16 [4096, 128], P(('groups', 'dp')), parts along dimension 0, may hold values from -3 to 3
- out_cotangent: bfloat16 [4096, 8192], P(('groups', 'dp')), parts along dimension 0, may hold values from -6 to 6
- prompt_states: bfloat16 [32, 8, 64, 128], P(('groups', 'dp')), parts along dimension 0, may hold values from -2 to 2
- prompt_tails: bfloat16 [32, 3, 576], P(('groups', 'dp')), parts along dimension 0, may hold values from -6 to 6
- rewards: float32 [32], P(('groups', 'dp')), parts along dimension 0, may hold values from 0 to 4
- lengths: int32 [32], P(('groups', 'dp')), parts along dimension 0, may hold values from 32 to 128, as said below
- owners: int32 [2, 16], P('groups'), parts along dimension 0, may hold values from 0 to 15, as said below
- conv_weight: float32 [4, 9216], replicated, may hold values from -3 to 3
- decay_log: float32 [128], replicated, may hold values from -7 to -2
- dt_bias: float32 [128], replicated, may hold values from -2 to 0
- skip_gain: float32 [128], replicated, may hold values from 0.5 to 1.5
Outputs:
- layer_output: bfloat16 [4096, 8192], P(('groups', 'dp')), parts along dimension 0
- state_grad: float32 [32, 8, 64, 128], P(('groups', 'dp')), parts along dimension 0
- tail_grad: float32 [32, 3, 576], P(('groups', 'dp')), parts along dimension 0
The draws below stay inside these ranges and needn't reach their ends.
There are 2 independent parts, one for each index of `groups`. The reference program is written for one: setup_inputs(seed, part) draws one part's arguments, and reference() takes and returns one part's arrays. A program takes and returns all parts, laid end to end along the dimension named above; an argument that names none is the same for every part. Nothing has to cross between parts.
Inputs may be any that keep to these rules, and one draw needn't show every extreme that they name: owners lists each of 0 to 15 once. `lengths`: some response has all 128 tokens.
All inputs are finite; a program needn't handle non-finite values.
Results may differ from the reference program's by a relative error of at most 0.0031.
Values may be sent and summed in bfloat16 or wider, within the bound.
A program may use at most 128 MiB of HBM per device.

```python
import jax
import jax.numpy as jnp
from jax import lax

H = 128
P_SIZE = 64
N = 128
G = 4
K = 4
RESP = 16
TOK_DEV = 128
LAGS = 3
HB = 8
CH = 9216
TW = 576
RESPONSES = 16
PROMPTS = 1
TOKENS = 2048


def draw_owners(key, part):
    key = jax.random.fold_in(key, 11)
    order = jax.random.permutation(key, RESPONSES).astype(jnp.int32)
    return order.reshape(PROMPTS, RESP)


def draw_lengths(key, part):
    key = jax.random.fold_in(key, 13)
    first_key, second_key = jax.random.split(key)
    base_len = jax.random.randint(first_key, (RESPONSES,), TOK_DEV // 4, TOK_DEV + 1).astype(jnp.int32)
    full_spot = jax.random.randint(second_key, (), 0, RESPONSES)
    return base_len.at[full_spot].set(TOK_DEV)


def steps_of(stream_key, dims, shards, least, largest):
    def one(position, parts):
        heights = jax.random.uniform(jax.random.fold_in(jax.random.fold_in(stream_key, 6), position), (parts,), jnp.float32, least / len(shards), largest / len(shards))
        return jnp.repeat(jnp.exp(heights), dims[position] // parts).reshape((-1,) + (1,) * (len(dims) - position - 1))

    gain = one(*shards[0])
    for cut in shards[1:]:
        gain = gain * one(*cut)
    return gain


def scatter_about(own_key, shape, width, reach, pieces=(), kind=jnp.bfloat16):
    values = jax.random.normal(own_key, shape, jnp.float32) * width
    if len(pieces) > 0:
        values = steps_of(own_key, shape, pieces, -0.22, 0.18) * values
    return jnp.clip(values, min=-reach, max=reach).astype(kind)


def setup_inputs(seed: int = 0, part: int = 0) -> dict:
    seeds = jax.random.split(jax.random.key(seed), 14)
    part_keys = jax.random.split(jax.random.fold_in(seeds[13], part), 14)
    return {
        "x_input": scatter_about(part_keys[0], (TOKENS, H * P_SIZE), 1.0, 6.0, ((0, 16),)),
        "bc_input": scatter_about(part_keys[1], (TOKENS, 2 * G * N), 0.5, 3.0, ((0, 16),)),
        "dt_input": scatter_about(part_keys[2], (TOKENS, H), 0.5, 3.0, ((0, 16),)),
        "out_cotangent": scatter_about(part_keys[3], (TOKENS, H * P_SIZE), 1.0, 6.0, ((0, 16),)),
        "prompt_states": scatter_about(part_keys[4], (RESPONSES, HB, P_SIZE, N), 0.3, 2.0, ((0, 16),)),
        "prompt_tails": scatter_about(part_keys[5], (RESPONSES, LAGS, TW), 1.0, 6.0, ((0, 16),)),
        "rewards": jnp.clip(4.0 * jax.random.uniform(part_keys[6], (RESPONSES,), jnp.float32) ** steps_of(part_keys[6], (RESPONSES,), ((0, 16),), -0.2, 0.2), 0.0, 4.0),
        "lengths": draw_lengths(jax.random.fold_in(jax.random.fold_in(seeds[13], part), 71), part),
        "owners": draw_owners(jax.random.fold_in(jax.random.fold_in(seeds[13], part), 71), part),
        "conv_weight": scatter_about(seeds[9], (K, CH), K ** -0.5, 3.0, (), jnp.float32),
        "decay_log": jnp.clip(jax.random.uniform(seeds[10], (H,), jnp.float32, -7.0, -2.0), -7.0, -2.0),
        "dt_bias": jnp.clip(jax.random.uniform(seeds[11], (H,), jnp.float32, -2.0, 0.0), -2.0, 0.0),
        "skip_gain": jnp.clip(jax.random.uniform(seeds[12], (H,), jnp.float32, 0.5, 1.5), 0.5, 1.5),
    }


highest = lax.Precision.HIGHEST

def local_layer(prompt_state, prompt_tail, x_rows, bc_rows, dt_rows, conv_weight, decay_log, dt_bias, skip_gain):
    steps_len = x_rows.shape[0]
    head_count, head_size, state_size = prompt_state.shape
    inner_width = head_count * head_size
    group_width = bc_rows.shape[1] // 2
    group_count = group_width // state_size
    per_group = head_count // group_count
    kernel = conv_weight.shape[0]
    joined = jnp.concatenate([prompt_tail, jnp.concatenate([x_rows, bc_rows], axis=1)], axis=0).astype(jnp.float32)
    conv_sum = conv_weight[0][None, :] * joined[0:steps_len]
    for offset in range(1, kernel):
        conv_sum = conv_sum + conv_weight[offset][None, :] * joined[offset:offset + steps_len]
    active = jax.nn.silu(conv_sum)
    values = active[:, :inner_width].reshape(steps_len, group_count, per_group, head_size)
    b_proj = active[:, inner_width:inner_width + group_width].reshape(steps_len, group_count, state_size)
    c_proj = active[:, inner_width + group_width:].reshape(steps_len, group_count, state_size)
    step_size = jax.nn.softplus(dt_rows.astype(jnp.float32) + dt_bias[None, :])
    cumulative = jnp.cumsum(-step_size * jnp.exp(decay_log)[None, :], axis=0)
    scores = jnp.einsum('tgn,sgn->gts', c_proj, b_proj, precision=highest)
    log_gap = cumulative.T[:, :, None] - cumulative.T[:, None, :]
    causal = jnp.arange(steps_len)[:, None] >= jnp.arange(steps_len)[None, :]
    decay_mask = jnp.where(causal[None], jnp.exp(jnp.minimum(log_gap, 0.0)), 0.0)
    mixing = decay_mask.reshape(group_count, per_group, steps_len, steps_len) * scores[:, None]
    mixing = mixing * step_size.T.reshape(group_count, per_group, 1, steps_len)
    within = jnp.einsum('gkts,sgkp->tgkp', mixing, values, precision=highest)
    state_wide = prompt_state.astype(jnp.float32).reshape(group_count, per_group, head_size, state_size)
    carried = jnp.einsum('tgn,gkpn->tgkp', c_proj, state_wide, precision=highest)
    carried = carried * jnp.exp(cumulative).reshape(steps_len, group_count, per_group, 1)
    result = within + carried + skip_gain.reshape(group_count, per_group)[None, :, :, None] * values
    return result.reshape(steps_len, inner_width)

def response_pass(prompt_state, prompt_tail, x_rows, bc_rows, dt_rows, seed_grad, conv_weight, decay_log, dt_bias, skip_gain):

    def forward(state_arg, tail_arg):
        return local_layer(state_arg, tail_arg, x_rows, bc_rows, dt_rows, conv_weight, decay_log, dt_bias, skip_gain)
    layer_out, pullback = jax.vjp(forward, prompt_state, prompt_tail)
    grad_state, grad_tail = pullback(seed_grad)
    return (layer_out.astype(jnp.bfloat16), grad_state.astype(jnp.bfloat16), grad_tail.astype(jnp.bfloat16))

def reference(x_input, bc_input, dt_input, out_cotangent, prompt_states, prompt_tails, rewards, lengths, owners, conv_weight, decay_log, dt_bias, skip_gain):
    inverse = jnp.zeros((RESPONSES,), jnp.int32).at[owners.reshape(-1)].set(jnp.arange(RESPONSES, dtype=jnp.int32))
    prompt_of = (inverse // RESP).astype(jnp.int32)
    slots = jnp.arange(PROMPTS, dtype=jnp.int32)
    member = (prompt_of[None, :] == slots[:, None]).astype(jnp.float32)
    means = lax.optimization_barrier(jnp.sum(member * rewards[None, :], axis=1)) / RESP
    spreads = lax.optimization_barrier(jnp.sum(member * (rewards[None, :] - means[:, None]) ** 2, axis=1)) / RESP
    advantage = (rewards - means[prompt_of]) / jnp.maximum(jnp.sqrt(spreads[prompt_of]), 1.0)
    positions = jnp.arange(TOK_DEV, dtype=jnp.int32)

    def single(index):
        chosen = prompt_of[index]
        holders = owners[chosen]
        prompt_state = jnp.take(prompt_states, holders, axis=0).reshape(H, P_SIZE, N)
        prompt_tail = jnp.take(prompt_tails, holders, axis=0).transpose(1, 0, 2).reshape(LAGS, CH)
        start = (index * TOK_DEV).astype(jnp.int32)
        x_rows = lax.dynamic_slice_in_dim(x_input, start, TOK_DEV)
        bc_rows = lax.dynamic_slice_in_dim(bc_input, start, TOK_DEV)
        dt_rows = lax.dynamic_slice_in_dim(dt_input, start, TOK_DEV)
        cot_rows = lax.dynamic_slice_in_dim(out_cotangent, start, TOK_DEV)
        length = lengths[index]
        alive = (positions < length).astype(jnp.float32)
        weight = advantage[index] * alive / length.astype(jnp.float32)
        seed_grad = cot_rows.astype(jnp.float32) * weight[:, None]
        return response_pass(prompt_state, prompt_tail, x_rows, bc_rows, dt_rows, seed_grad, conv_weight, decay_log, dt_bias, skip_gain)
    outputs, state_grads, tail_grads = lax.map(single, jnp.arange(RESPONSES, dtype=jnp.int32))
    per_prompt = jnp.einsum('pr,rx->px', member, state_grads.reshape(RESPONSES, -1).astype(jnp.float32), precision=highest)
    state_out = per_prompt.reshape(PROMPTS * RESP, HB, P_SIZE, N)[inverse]
    tail_prompt = jnp.einsum('pr,rx->px', member, tail_grads.reshape(RESPONSES, -1).astype(jnp.float32), precision=highest)
    tail_out = tail_prompt.reshape(PROMPTS, LAGS, RESP, TW).transpose(0, 2, 1, 3).reshape(PROMPTS * RESP, LAGS, TW)[inverse]
    return (outputs.reshape(TOKENS, H * P_SIZE), state_out, tail_out)
```

```python
import jax
import jax.numpy as jnp
from jax import lax
from jax.experimental import pallas as pl
from jax.experimental.pallas import tpu as pltpu
from jax.sharding import PartitionSpec as P

highest = lax.Precision.HIGHEST
f32 = jnp.float32
bf16 = jnp.bfloat16


def split(a):
    hi = a.astype(bf16)
    return hi, (a - hi.astype(f32)).astype(bf16)


def dot(a, b, dims):
    return lax.dot_general(a, b, (dims, ((), ())), preferred_element_type=f32)


def widen(cols, head_size):
    rows, heads = cols.shape
    return jnp.concatenate(
        [jnp.broadcast_to(cols[:, h : h + 1], (rows, head_size)) for h in range(heads)], axis=1
    )


def within_kernel(
    blocks_per_group, head_size, lags, own, x_ref, cot_ref, tail_ref, conv_ref, cumc_ref, cumr_ref,
    delr_ref, wt_ref, skip_ref, score_ref, cc_ref, y_ref, dst_ref, dtail_ref, dscore_ref, ext,
):
    j = pl.program_id(0)
    rows = x_ref.shape[0]
    heads = cumc_ref.shape[2]
    state_size = score_ref.shape[2]
    ext[0:8, :] = tail_ref[...]
    ext[8:, :] = x_ref[...].astype(f32)
    conv = conv_ref[...]
    u = conv[0:1] * ext[8 - lags : 8 - lags + rows, :]
    for k in range(1, lags + 1):
        u = u + conv[k : k + 1] * ext[8 - lags + k : 8 - lags + k + rows, :]
    sig = 1.0 / (1.0 + jnp.exp(-u))
    act = u * sig
    act_hi, act_lo = split(act)
    cumc = cumc_ref[0]
    weight = wt_ref[...]
    score = score_ref[0]
    cot = cot_ref[...]
    parts, dvals = [], []
    dscore = jnp.zeros((rows, 8), f32)
    for h in range(heads):
        lanes = slice(h * head_size, (h + 1) * head_size)
        gap = cumc[:, h : h + 1] - cumr_ref[0, h : h + 1, :]
        decay = jnp.exp(jnp.minimum(gap, 0.0)) * delr_ref[0, h : h + 1, :]
        mix = decay * score
        mix_hi, mix_lo = split(mix)
        hi, lo = act_hi[:, lanes], act_lo[:, lanes]
        wide = dot(mix_hi, jnp.concatenate([hi, lo], axis=1), ((1,), (0,)))
        part = wide[:, :head_size] + wide[:, head_size:] + dot(mix_lo, hi, ((1,), (0,)))
        parts.append(part)
        mw_hi, mw_lo = split(mix[:, :8] * weight)
        cot_h = cot[:, lanes]
        both = dot(jnp.concatenate([mw_hi, mw_lo], axis=1), cot_h, ((0,), (0,)))
        dvals.append(both[:8] + both[8:])
        q = dot(cot_h, hi[:8], ((1,), (1,))) + dot(cot_h, lo[:8], ((1,), (1,)))
        dscore = dscore + decay[:, :8] * q
    skip = skip_ref[...]
    y_ref[...] = jnp.concatenate(parts, axis=1) + skip * act
    dscore = dscore * weight

    @pl.when(lax.rem(j, blocks_per_group) == 0)
    def _():
        dscore_ref[0] = dscore

    @pl.when(lax.rem(j, blocks_per_group) != 0)
    def _():
        dscore_ref[0] += dscore

    cot32 = cot.astype(f32)
    z_hi, z_lo = split(cot32 * widen(jnp.exp(cumc) * weight, head_size))
    cc = cc_ref[0]
    wide = dot(z_hi, cc, ((0,), (0,)))
    dst = wide[:, :state_size] + wide[:, state_size:] + dot(z_lo, cc[:, :state_size], ((0,), (0,)))
    dst_ref[0] = dst.astype(bf16)

    dact = jnp.concatenate(dvals, axis=1) + skip * cot32[:8] * weight[:8]
    u8, s8 = u[:8], sig[:8]
    dtail_ref[...] = dact * (s8 * (1.0 + u8 * (1.0 - s8)))


def carried_kernel(
    blocks_per_group, head_size, own, y_ref, cot_ref, cumc_ref, wt_ref, cc_ref, state_ref, out_ref, dc_ref
):
    j = pl.program_id(0)
    state_size = state_ref.shape[2]
    state = state_ref[0]
    cc = cc_ref[0]
    carried = dot(cc[:, :state_size], state, ((1,), (1,))) + dot(
        cc[:, state_size:], state, ((1,), (1,))
    )
    gains = jnp.exp(cumc_ref[0])
    wide = widen(gains, head_size)
    out_ref[...] = (y_ref[...] + wide * carried).astype(bf16)
    z = cot_ref[...][:8].astype(f32) * (wide[:8] * wt_ref[...][:8])
    z_hi, z_lo = split(z)
    dc = dot(z_hi, state, ((1,), (0,))) + dot(z_lo, state, ((1,), (0,)))

    @pl.when(lax.rem(j, blocks_per_group) == 0)
    def _():
        dc_ref[0] = dc

    @pl.when(lax.rem(j, blocks_per_group) != 0)
    def _():
        dc_ref[0] += dc


def spread(a, count):
    return lax.all_to_all(
        jnp.broadcast_to(a[None], (count,) + a.shape), "dp", split_axis=0, concat_axis=0, tiled=True
    )


def local(
    x_input, bc_input, dt_input, out_cotangent, prompt_states, prompt_tails, rewards, lengths,
    owners, conv_weight, decay_log, dt_bias, skip_gain,
):
    device_count = lax.axis_size("dp")
    my_index = lax.axis_index("dp")
    prompt_count, resp_count = owners.shape
    _, block_heads, head_size, state_size = prompt_states.shape
    lags, tail_width = prompt_tails.shape[1:]
    rows, inner = x_input.shape
    heads = dt_input.shape[1]
    group_width = bc_input.shape[1] // 2
    groups = group_width // state_size
    width = block_heads * head_size
    per_group = resp_count // groups
    tail_len = lags * tail_width
    holder_ids = jnp.arange(device_count, dtype=jnp.int32)
    prompt_ids = jnp.arange(prompt_count, dtype=jnp.int32)

    small = jnp.concatenate([prompt_tails.reshape(-1).astype(f32), rewards.astype(f32)])
    small = spread(jnp.pad(small, (0, -small.shape[0] % 128)), device_count)
    states = spread(prompt_states.reshape(width, state_size), device_count)

    matches = owners[:, :, None] == holder_ids[None, None, :]
    held_prompt = jnp.sum(jnp.where(matches, prompt_ids[:, None, None], 0), axis=(0, 1))
    my_prompt = jnp.sum(jnp.where(holder_ids == my_index, held_prompt, 0))
    owner_row = jnp.sum(jnp.where((prompt_ids == my_prompt)[:, None], owners, 0), axis=0)
    pick = (owner_row[:, None] == holder_ids[None, :]).astype(f32)

    member = (held_prompt == my_prompt).astype(f32)
    reward_all = small[:, tail_len]
    mean_value = jnp.sum(member * reward_all) / resp_count
    spread_value = jnp.sum(member * (reward_all - mean_value) ** 2) / resp_count
    advantage = (rewards[0] - mean_value) / jnp.maximum(jnp.sqrt(spread_value), 1.0)
    length = lengths[0]
    alive = (jnp.arange(rows, dtype=jnp.int32) < length).astype(f32)
    weight = (advantage * alive / length.astype(f32))[:, None]

    tails = jnp.dot(pick, small[:, :tail_len], precision=highest)
    tails = tails.reshape(resp_count, lags, tail_width).transpose(1, 0, 2).reshape(lags, -1)

    bc_ext = jnp.concatenate([tails[:, inner:], bc_input.astype(f32)], axis=0)
    bc_conv = conv_weight[:, inner:]
    bc_u = bc_conv[0][None] * bc_ext[0:rows]
    for k in range(1, lags + 1):
        bc_u = bc_u + bc_conv[k][None] * bc_ext[k : k + rows]
    bc_act = jax.nn.silu(bc_u)
    b_proj = bc_act[:, :group_width].reshape(rows, groups, state_size)
    c_proj = bc_act[:, group_width:].reshape(rows, groups, state_size)
    causal = jnp.arange(rows)[:, None] >= jnp.arange(rows)[None, :]
    scores = jnp.einsum("tgn,sgn->gts", c_proj, b_proj, precision=highest)
    scores = jnp.where(causal[None], scores, 0.0)
    c_group = c_proj.transpose(1, 0, 2)
    c_hi, c_lo = split(c_group)
    cc = jnp.concatenate([c_hi, c_lo], axis=2)

    step_size = jax.nn.softplus(dt_input.astype(f32) + dt_bias[None, :])
    decrement = -step_size * jnp.exp(decay_log)[None, :]
    cumulative = jnp.dot(causal.astype(f32), decrement, precision=highest)
    cumc = cumulative.reshape(rows, resp_count, block_heads).transpose(1, 0, 2)
    cumr = cumulative.T.reshape(resp_count, block_heads, rows)
    delr = step_size.T.reshape(resp_count, block_heads, rows)
    skip = jnp.repeat(skip_gain, head_size)[None, :]
    tail8 = jnp.pad(tails[:, :inner], ((8 - lags, 0), (0, 0)))
    conv_x = conv_weight[:, :inner]
    taps = conv_x.shape[0]

    wide_spec = pl.BlockSpec((rows, width), lambda j, own: (0, j))
    cumc_spec = pl.BlockSpec((1, rows, block_heads), lambda j, own: (j, 0, 0))
    row_spec = pl.BlockSpec((1, block_heads, rows), lambda j, own: (j, 0, 0))
    wt_spec = pl.BlockSpec((rows, 1), lambda j, own: (0, 0))
    cc_spec = pl.BlockSpec((1, rows, 2 * state_size), lambda j, own: (j // per_group, 0, 0))
    slot_spec = pl.BlockSpec((1, width, state_size), lambda j, own: (own[j], 0, 0))
    eight = pl.BlockSpec((8, width), lambda j, own: (0, j))

    y_part, dstate, du_x, dscore = pl.pallas_call(
        lambda *refs: within_kernel(per_group, head_size, lags, *refs),
        grid_spec=pltpu.PrefetchScalarGridSpec(
            num_scalar_prefetch=1,
            grid=(resp_count,),
            in_specs=[
                wide_spec,
                wide_spec,
                eight,
                pl.BlockSpec((taps, width), lambda j, own: (0, j)),
                cumc_spec,
                row_spec,
                row_spec,
                wt_spec,
                pl.BlockSpec((1, width), lambda j, own: (0, j)),
                pl.BlockSpec((1, rows, rows), lambda j, own: (j // per_group, 0, 0)),
                cc_spec,
            ],
            out_specs=[
                wide_spec,
                slot_spec,
                eight,
                pl.BlockSpec((1, rows, 8), lambda j, own: (j // per_group, 0, 0)),
            ],
            scratch_shapes=[pltpu.VMEM((rows + 8, width), f32)],
        ),
        out_shape=[
            jax.ShapeDtypeStruct((rows, inner), f32),
            jax.ShapeDtypeStruct((device_count, width, state_size), bf16),
            jax.ShapeDtypeStruct((8, inner), f32),
            jax.ShapeDtypeStruct((groups, rows, 8), f32),
        ],
        compiler_params=pltpu.CompilerParams(vmem_limit_bytes=24 << 20),
        cost_estimate=pl.CostEstimate(flops=3 << 30, bytes_accessed=12 << 20, transcendentals=4 << 20),
        name="within",
    )(owner_row, x_input, out_cotangent, tail8, conv_x, cumc, cumr, delr, weight, skip, scores, cc)

    if prompt_count > 1:
        dstate = jnp.where((held_prompt == my_prompt)[:, None, None], dstate, jnp.zeros_like(dstate))
    got = lax.all_to_all(dstate, "dp", split_axis=0, concat_axis=0, tiled=True)

    layer_out, dc_state = pl.pallas_call(
        lambda *refs: carried_kernel(per_group, head_size, *refs),
        grid_spec=pltpu.PrefetchScalarGridSpec(
            num_scalar_prefetch=1,
            grid=(resp_count,),
            in_specs=[wide_spec, pl.BlockSpec((16, width), lambda j, own: (0, j)), cumc_spec, wt_spec, cc_spec, slot_spec],
            out_specs=[
                wide_spec,
                pl.BlockSpec((1, 8, state_size), lambda j, own: (j // per_group, 0, 0)),
            ],
        ),
        out_shape=[
            jax.ShapeDtypeStruct((rows, inner), bf16),
            jax.ShapeDtypeStruct((groups, 8, state_size), f32),
        ],
        compiler_params=pltpu.CompilerParams(vmem_limit_bytes=24 << 20),
        cost_estimate=pl.CostEstimate(flops=1 << 30, bytes_accessed=9 << 20, transcendentals=1 << 17),
        name="carried",
    )(owner_row, y_part, out_cotangent, cumc, weight, cc, states)

    keep = jnp.where(causal[:, :8][None], dscore, 0.0)
    db = jnp.einsum("gts,gtn->sgn", keep, c_group, precision=highest).reshape(8, group_width)
    dc = jnp.einsum("gts,sgn->tgn", keep[:, :8], b_proj[:8], precision=highest)
    dc = (dc + dc_state.transpose(1, 0, 2)).reshape(8, group_width)
    sig = jax.nn.sigmoid(bc_u[:8])
    du_bc = jnp.concatenate([db, dc], axis=1) * (sig * (1.0 + bc_u[:8] * (1.0 - sig)))
    du = jnp.concatenate([du_x, du_bc], axis=1)
    dtail = jnp.stack(
        [sum(conv_weight[m - t] * du[t] for t in range(m + 1)) for m in range(lags)]
    ).astype(bf16)
    tail_blocks = dtail.reshape(lags, resp_count, tail_width).transpose(1, 0, 2)
    tail_blocks = tail_blocks.reshape(resp_count, tail_len)
    tail_send = jnp.dot(pick.T.astype(bf16), tail_blocks, preferred_element_type=f32).astype(bf16)
    got_tail = lax.all_to_all(tail_send, "dp", split_axis=0, concat_axis=0, tiled=True)

    state_grad = jnp.sum(got.astype(f32), axis=0)
    state_grad = state_grad.reshape(1, block_heads, head_size, state_size)
    tail_grad = jnp.sum(got_tail.astype(f32), axis=0).reshape(1, lags, tail_width)
    return layer_out, state_grad, tail_grad


def solution(mesh):
    in_specs = (
        P(("groups", "dp"), None),
        P(("groups", "dp"), None),
        P(("groups", "dp"), None),
        P(("groups", "dp"), None),
        P(("groups", "dp"), None, None, None),
        P(("groups", "dp"), None, None),
        P(("groups", "dp")),
        P(("groups", "dp")),
        P("groups", None),
        P(),
        P(),
        P(),
        P(),
    )
    out_specs = (
        P(("groups", "dp"), None),
        P(("groups", "dp"), None, None, None),
        P(("groups", "dp"), None, None),
    )
    return jax.shard_map(local, mesh=mesh, in_specs=in_specs, out_specs=out_specs, check_vma=False)
```

```python
import jax
import jax.numpy as jnp
from jax import lax
from jax.experimental import pallas as pl
from jax.experimental.pallas import tpu as pltpu
from jax.sharding import PartitionSpec as P

highest = lax.Precision.HIGHEST
f32 = jnp.float32
bf16 = jnp.bfloat16


def split(a):
    hi = a.astype(bf16)
    return hi, (a - hi.astype(f32)).astype(bf16)


def dot(a, b, dims):
    return lax.dot_general(a, b, (dims, ((), ())), preferred_element_type=f32)


def widen(cols, head_size):
    rows, heads = cols.shape
    return jnp.concatenate(
        [jnp.broadcast_to(cols[:, h : h + 1], (rows, head_size)) for h in range(heads)], axis=1
    )


def exchange_kernel(count, src_ref, out_ref, send_sem, recv_sem, own_sem):
    me = lax.axis_index("dp")
    barrier = pltpu.get_barrier_semaphore()

    def greet(step, carry):
        peer = lax.rem(me + step, count)
        pl.semaphore_signal(
            barrier, inc=1, device_id={"dp": peer}, device_id_type=pl.DeviceIdType.MESH
        )
        return carry

    lax.fori_loop(1, count, greet, 0)
    pl.semaphore_wait(barrier, count - 1)

    def copy(step):
        peer = lax.rem(me + step, count)
        return pltpu.make_async_remote_copy(
            src_ref=src_ref.at[peer],
            dst_ref=out_ref.at[me],
            send_sem=send_sem.at[step],
            recv_sem=recv_sem.at[step],
            device_id={"dp": peer},
            device_id_type=pl.DeviceIdType.MESH,
        )

    def start(step, carry):
        copy(step).start()
        return carry

    def finish(step, carry):
        copy(step).wait()
        return carry

    lax.fori_loop(1, count, start, 0)
    mine = pltpu.make_async_copy(src_ref.at[me], out_ref.at[me], own_sem)
    mine.start()
    mine.wait()
    lax.fori_loop(1, count, finish, 0)


def exchange(a, count, collective_id):
    return pl.pallas_call(
        lambda *refs: exchange_kernel(count, *refs),
        out_shape=jax.ShapeDtypeStruct(a.shape, a.dtype),
        in_specs=[pl.BlockSpec(memory_space=pltpu.VMEM)],
        out_specs=pl.BlockSpec(memory_space=pltpu.VMEM),
        scratch_shapes=[
            pltpu.SemaphoreType.DMA((count,)),
            pltpu.SemaphoreType.DMA((count,)),
            pltpu.SemaphoreType.DMA,
        ],
        compiler_params=pltpu.CompilerParams(
            collective_id=collective_id, has_side_effects=True, vmem_limit_bytes=16 << 20
        ),
        cost_estimate=pl.CostEstimate(flops=0, bytes_accessed=12 << 20, transcendentals=0),
        name="exchange",
    )(a)


def prepare_kernel(
    groups, state_size, lags, dt_ref, bias_ref, decay_ref, bc_ref, tail_ref, conv_ref,
    cum_ref, step_ref, score_ref, scoret_ref, cc_ref, act_ref, u8_ref, ext,
):
    rows = dt_ref.shape[0]
    row = lax.broadcasted_iota(jnp.int32, (rows, rows), 0)
    col = lax.broadcasted_iota(jnp.int32, (rows, rows), 1)
    logits = dt_ref[...].astype(f32) + bias_ref[...]
    step = jnp.maximum(logits, 0.0) + jnp.log1p(jnp.exp(-jnp.abs(logits)))
    dec = -step * jnp.exp(decay_ref[...])
    step_ref[...] = step.T
    cum_ref[...] = lax.dot_general(
        dec.T, jnp.where(row <= col, 1.0, 0.0), (((1,), (0,)), ((), ())),
        precision=highest, preferred_element_type=f32,
    )
    ext[0:8, :] = tail_ref[...]
    ext[8:, :] = bc_ref[...].astype(f32)
    conv = conv_ref[...]
    u = conv[0:1] * ext[8 - lags : 8 - lags + rows, :]
    for k in range(1, lags + 1):
        u = u + conv[k : k + 1] * ext[8 - lags + k : 8 - lags + k + rows, :]
    u8_ref[...] = u[:8]
    act = u * (1.0 / (1.0 + jnp.exp(-u)))
    act_ref[...] = act
    for g in range(groups):
        b = act[:, g * state_size : (g + 1) * state_size]
        c = act[:, (groups + g) * state_size : (groups + g + 1) * state_size]
        score = lax.dot_general(
            c, b, (((1,), (1,)), ((), ())), precision=highest, preferred_element_type=f32
        )
        score = jnp.where(row >= col, score, 0.0)
        score_ref[g] = score
        scoret_ref[g] = score.T[:8]
        hi, lo = split(c)
        cc_ref[g, :, :state_size] = hi
        cc_ref[g, :, state_size:] = lo


def within_kernel(
    blocks_per_group, head_size, lags, own, x_ref, cot_ref, tail_ref, conv_ref, cumr_ref,
    delr_ref, wt_ref, wrow_ref, skip_ref, score_ref, scoret_ref, cc_ref, y_ref, dst_ref, dtail_ref, dscore_ref, ext,
):
    j = pl.program_id(0)
    rows = x_ref.shape[0]
    heads = cumr_ref.shape[0]
    state_size = cc_ref.shape[2] // 2
    ext[0:8, :] = tail_ref[...]
    ext[8:, :] = x_ref[...].astype(f32)
    conv = conv_ref[...]
    u = conv[0:1] * ext[8 - lags : 8 - lags + rows, :]
    for k in range(1, lags + 1):
        u = u + conv[k : k + 1] * ext[8 - lags + k : 8 - lags + k + rows, :]
    sig = 1.0 / (1.0 + jnp.exp(-u))
    act = u * sig
    act_hi, act_lo = split(act)
    cumr = cumr_ref[...]
    delr = delr_ref[...]
    cumc = cumr.T
    delc8 = delr.T[:8]
    weight = wt_ref[...]
    wrow = wrow_ref[...]
    score = score_ref[0]
    score_t = scoret_ref[0] * wrow
    cot = cot_ref[...]
    pair = 2 * head_size
    first = lax.broadcasted_iota(jnp.int32, (1, pair), 1) < head_size
    parts, dvals = [], []
    dscore = jnp.zeros((8, rows), f32)
    for p in range(heads // 2):
        lanes = slice(p * pair, (p + 1) * pair)
        lhs, grads, decays = [], [], []
        for h in (2 * p, 2 * p + 1):
            gap = cumc[:, h : h + 1] - cumr[h : h + 1, :]
            mix = jnp.exp(jnp.minimum(gap, 0.0)) * delr[h : h + 1, :] * score
            lhs.extend(split(mix))
            gap8 = cumr[h : h + 1, :] - cumc[:8, h : h + 1]
            decay8 = jnp.exp(jnp.minimum(gap8, 0.0)) * delc8[:, h : h + 1]
            decays.append(decay8)
            mix8 = decay8 * score_t
            hi8 = mix8.astype(bf16).astype(f32)
            grads.extend([hi8, mix8 - hi8])
        wide = dot(
            jnp.concatenate(lhs, axis=0),
            jnp.concatenate([act_hi[:, lanes], act_lo[:, lanes]], axis=1),
            ((1,), (0,)),
        )
        even = wide[:rows, :pair] + wide[:rows, pair:] + wide[rows : 2 * rows, :pair]
        odd = wide[2 * rows : 3 * rows, :pair] + wide[2 * rows : 3 * rows, pair:] + wide[3 * rows :, :pair]
        parts.append(jnp.where(first, even, odd))
        cot_p = cot[:, lanes]
        both = dot(jnp.concatenate(grads, axis=0).astype(bf16), cot_p, ((1,), (0,)))
        dvals.append(jnp.where(first, both[:8] + both[8:16], both[16:24] + both[24:]))
        a8 = act[:8, lanes]
        h8 = a8.astype(bf16).astype(f32)
        l8 = a8 - h8
        zero = jnp.zeros_like(a8)
        picks = jnp.concatenate(
            [jnp.where(first, h8, zero), jnp.where(first, l8, zero),
             jnp.where(first, zero, h8), jnp.where(first, zero, l8)], axis=0,
        ).astype(bf16)
        q = dot(picks, cot_p, ((1,), (1,)))
        dscore = dscore + decays[0] * (q[:8] + q[8:16]) + decays[1] * (q[16:24] + q[24:])
    skip = skip_ref[...]
    y_ref[...] = jnp.concatenate(parts, axis=1) + skip * act
    dscore = dscore * wrow

    @pl.when(lax.rem(j, blocks_per_group) == 0)
    def _():
        dscore_ref[0] = dscore

    @pl.when(lax.rem(j, blocks_per_group) != 0)
    def _():
        dscore_ref[0] += dscore

    cot32 = cot.astype(f32)
    z_hi, z_lo = split(cot32 * widen(jnp.exp(cumc) * weight, head_size))
    cc = cc_ref[0]
    wide = dot(z_hi, cc, ((0,), (0,)))
    dst = wide[:, :state_size] + wide[:, state_size:] + dot(z_lo, cc[:, :state_size], ((0,), (0,)))
    dst_ref[0] = dst.astype(bf16)

    dact = jnp.concatenate(dvals, axis=1) + skip * cot32[:8] * weight[:8]
    u8, s8 = u[:8], sig[:8]
    dtail_ref[...] = dact * (s8 * (1.0 + u8 * (1.0 - s8)))


def carried_kernel(
    blocks_per_group, head_size, own, y_ref, cot_ref, cumr_ref, wt_ref, cc_ref, state_ref, out_ref, dc_ref
):
    j = pl.program_id(0)
    state_size = state_ref.shape[2]
    state = state_ref[0]
    cc = cc_ref[0]
    carried = dot(cc[:, :state_size], state, ((1,), (1,))) + dot(
        cc[:, state_size:], state, ((1,), (1,))
    )
    gains = jnp.exp(cumr_ref[...]).T
    wide = widen(gains, head_size)
    out_ref[...] = (y_ref[...] + wide * carried).astype(bf16)
    z = cot_ref[...][:8].astype(f32) * (wide[:8] * wt_ref[...][:8])
    z_hi, z_lo = split(z)
    dc = dot(z_hi, state, ((1,), (0,))) + dot(z_lo, state, ((1,), (0,)))

    @pl.when(lax.rem(j, blocks_per_group) == 0)
    def _():
        dc_ref[0] = dc

    @pl.when(lax.rem(j, blocks_per_group) != 0)
    def _():
        dc_ref[0] += dc


def spread(a, count):
    return lax.all_to_all(
        jnp.broadcast_to(a[None], (count,) + a.shape), "dp", split_axis=0, concat_axis=0, tiled=True
    )


def local(
    x_input, bc_input, dt_input, out_cotangent, prompt_states, prompt_tails, rewards, lengths,
    owners, conv_weight, decay_log, dt_bias, skip_gain,
):
    device_count = lax.axis_size("dp")
    my_index = lax.axis_index("dp")
    prompt_count, resp_count = owners.shape
    _, block_heads, head_size, state_size = prompt_states.shape
    lags, tail_width = prompt_tails.shape[1:]
    rows, inner = x_input.shape
    heads = dt_input.shape[1]
    group_width = bc_input.shape[1] // 2
    groups = group_width // state_size
    width = block_heads * head_size
    per_group = resp_count // groups
    tail_len = lags * tail_width
    holder_ids = jnp.arange(device_count, dtype=jnp.int32)
    prompt_ids = jnp.arange(prompt_count, dtype=jnp.int32)

    small = jnp.concatenate([prompt_tails.reshape(-1).astype(f32), rewards.astype(f32)])
    small = jnp.pad(small, (0, -small.shape[0] % 1024)).reshape(1, -1, 128)
    small = jnp.broadcast_to(small, (device_count,) + small.shape[1:])
    small = exchange(small, device_count, 1).reshape(device_count, -1)
    states = spread(prompt_states.reshape(width, state_size), device_count)

    matches = owners[:, :, None] == holder_ids[None, None, :]
    held_prompt = jnp.sum(jnp.where(matches, prompt_ids[:, None, None], 0), axis=(0, 1))
    my_prompt = jnp.sum(jnp.where(holder_ids == my_index, held_prompt, 0))
    owner_row = jnp.sum(jnp.where((prompt_ids == my_prompt)[:, None], owners, 0), axis=0)
    pick = (owner_row[:, None] == holder_ids[None, :]).astype(f32)

    member = (held_prompt == my_prompt).astype(f32)
    reward_all = small[:, tail_len]
    mean_value = jnp.sum(member * reward_all) / resp_count
    spread_value = jnp.sum(member * (reward_all - mean_value) ** 2) / resp_count
    advantage = (rewards[0] - mean_value) / jnp.maximum(jnp.sqrt(spread_value), 1.0)
    length = lengths[0]
    alive = (jnp.arange(rows, dtype=jnp.int32) < length).astype(f32)
    weight = (advantage * alive / length.astype(f32))[:, None]

    tails = jnp.dot(pick, small[:, :tail_len], precision=highest)
    tails = tails.reshape(resp_count, lags, tail_width).transpose(1, 0, 2).reshape(lags, -1)

    tail8 = jnp.pad(tails, ((8 - lags, 0), (0, 0)))
    causal = jnp.arange(rows)[:, None] >= jnp.arange(rows)[None, :]
    cumr, delr, scores, scores_t, cc, bc_act, bc_u = pl.pallas_call(
        lambda *refs: prepare_kernel(groups, state_size, lags, *refs),
        out_shape=[
            jax.ShapeDtypeStruct((heads, rows), f32),
            jax.ShapeDtypeStruct((heads, rows), f32),
            jax.ShapeDtypeStruct((groups, rows, rows), f32),
            jax.ShapeDtypeStruct((groups, 8, rows), f32),
            jax.ShapeDtypeStruct((groups, rows, 2 * state_size), bf16),
            jax.ShapeDtypeStruct((rows, 2 * group_width), f32),
            jax.ShapeDtypeStruct((8, 2 * group_width), f32),
        ],
        scratch_shapes=[pltpu.VMEM((rows + 8, 2 * group_width), f32)],
        compiler_params=pltpu.CompilerParams(vmem_limit_bytes=24 << 20),
        name="prepare",
    )(dt_input, dt_bias[None, :], decay_log[None, :], bc_input, tail8[:, inner:], conv_weight[:, inner:])
    b_proj = bc_act[:, :group_width].reshape(rows, groups, state_size)
    c_proj = bc_act[:, group_width:].reshape(rows, groups, state_size)
    skip = jnp.repeat(skip_gain, head_size)[None, :]
    taps = conv_weight.shape[0]

    wide_spec = pl.BlockSpec((rows, width), lambda j, own: (0, j))
    row_spec = pl.BlockSpec((block_heads, rows), lambda j, own: (j, 0))
    wt_spec = pl.BlockSpec((rows, 1), lambda j, own: (0, 0))
    cc_spec = pl.BlockSpec((1, rows, 2 * state_size), lambda j, own: (j // per_group, 0, 0))
    slot_spec = pl.BlockSpec((1, width, state_size), lambda j, own: (own[j], 0, 0))
    eight = pl.BlockSpec((8, width), lambda j, own: (0, j))

    y_part, dstate, du_x, dscore = pl.pallas_call(
        lambda *refs: within_kernel(per_group, head_size, lags, *refs),
        grid_spec=pltpu.PrefetchScalarGridSpec(
            num_scalar_prefetch=1,
            grid=(resp_count,),
            in_specs=[
                wide_spec,
                wide_spec,
                eight,
                pl.BlockSpec((taps, width), lambda j, own: (0, j)),
                row_spec,
                row_spec,
                wt_spec,
                pl.BlockSpec((1, rows), lambda j, own: (0, 0)),
                pl.BlockSpec((1, width), lambda j, own: (0, j)),
                pl.BlockSpec((1, rows, rows), lambda j, own: (j // per_group, 0, 0)),
                pl.BlockSpec((1, 8, rows), lambda j, own: (j // per_group, 0, 0)),
                cc_spec,
            ],
            out_specs=[
                wide_spec,
                slot_spec,
                eight,
                pl.BlockSpec((1, 8, rows), lambda j, own: (j // per_group, 0, 0)),
            ],
            scratch_shapes=[pltpu.VMEM((rows + 8, width), f32)],
        ),
        out_shape=[
            jax.ShapeDtypeStruct((rows, inner), f32),
            jax.ShapeDtypeStruct((device_count, width, state_size), bf16),
            jax.ShapeDtypeStruct((8, inner), f32),
            jax.ShapeDtypeStruct((groups, 8, rows), f32),
        ],
        compiler_params=pltpu.CompilerParams(vmem_limit_bytes=24 << 20),
        cost_estimate=pl.CostEstimate(flops=3 << 30, bytes_accessed=12 << 20, transcendentals=4 << 20),
        name="within",
    )(owner_row, x_input, out_cotangent, tail8, conv_weight, cumr, delr, weight, weight.T, skip, scores, scores_t, cc)

    if prompt_count > 1:
        dstate = jnp.where((held_prompt == my_prompt)[:, None, None], dstate, jnp.zeros_like(dstate))
    got = lax.all_to_all(dstate, "dp", split_axis=0, concat_axis=0, tiled=True)

    layer_out, dc_state = pl.pallas_call(
        lambda *refs: carried_kernel(per_group, head_size, *refs),
        grid_spec=pltpu.PrefetchScalarGridSpec(
            num_scalar_prefetch=1,
            grid=(resp_count,),
            in_specs=[wide_spec, pl.BlockSpec((16, width), lambda j, own: (0, j)), row_spec, wt_spec, cc_spec, slot_spec],
            out_specs=[
                wide_spec,
                pl.BlockSpec((1, 8, state_size), lambda j, own: (j // per_group, 0, 0)),
            ],
        ),
        out_shape=[
            jax.ShapeDtypeStruct((rows, inner), bf16),
            jax.ShapeDtypeStruct((groups, 8, state_size), f32),
        ],
        compiler_params=pltpu.CompilerParams(vmem_limit_bytes=24 << 20),
        cost_estimate=pl.CostEstimate(flops=1 << 30, bytes_accessed=9 << 20, transcendentals=1 << 17),
        name="carried",
    )(owner_row, y_part, out_cotangent, cumr, weight, cc, states)

    keep = jnp.where(causal[:, :8].T[None], dscore, 0.0)
    db = jnp.einsum("gst,tgn->sgn", keep, c_proj, precision=highest).reshape(8, group_width)
    dc = jnp.einsum("gst,sgn->tgn", keep[:, :, :8], b_proj[:8], precision=highest)
    dc = (dc + dc_state.transpose(1, 0, 2)).reshape(8, group_width)
    sig = jax.nn.sigmoid(bc_u[:8])
    du_bc = jnp.concatenate([db, dc], axis=1) * (sig * (1.0 + bc_u[:8] * (1.0 - sig)))
    du = jnp.concatenate([du_x, du_bc], axis=1)
    dtail = jnp.stack(
        [sum(conv_weight[m - t] * du[t] for t in range(m + 1)) for m in range(lags)]
    ).astype(bf16)
    tail_blocks = dtail.reshape(lags, resp_count, tail_width).transpose(1, 0, 2)
    tail_blocks = tail_blocks.reshape(resp_count, tail_len)
    tail_send = jnp.dot(pick.T.astype(bf16), tail_blocks, preferred_element_type=f32).astype(bf16)
    tail_send = jnp.pad(tail_send, ((0, 0), (0, -tail_len % 2048))).reshape(device_count, -1, 128)
    got_tail = exchange(tail_send, device_count, 2).reshape(device_count, -1)[:, :tail_len]

    state_grad = jnp.sum(got.astype(f32), axis=0)
    state_grad = state_grad.reshape(1, block_heads, head_size, state_size)
    tail_grad = jnp.sum(got_tail.astype(f32), axis=0).reshape(1, lags, tail_width)
    return layer_out, state_grad, tail_grad


def solution(mesh):
    in_specs = (
        P(("groups", "dp"), None),
        P(("groups", "dp"), None),
        P(("groups", "dp"), None),
        P(("groups", "dp"), None),
        P(("groups", "dp"), None, None, None),
        P(("groups", "dp"), None, None),
        P(("groups", "dp")),
        P(("groups", "dp")),
        P("groups", None),
        P(),
        P(),
        P(),
        P(),
    )
    out_specs = (
        P(("groups", "dp"), None),
        P(("groups", "dp"), None, None, None),
        P(("groups", "dp"), None, None),
    )
    return jax.shard_map(local, mesh=mesh, in_specs=in_specs, out_specs=out_specs, check_vma=False)
```

```python
import jax
import jax.numpy as jnp
from jax import lax
from jax.experimental import pallas as pl
from jax.experimental.pallas import tpu as pltpu
from jax.sharding import PartitionSpec as P

highest = lax.Precision.HIGHEST
f32 = jnp.float32
bf16 = jnp.bfloat16


def split(a):
    hi = a.astype(bf16)
    return hi, (a - hi.astype(f32)).astype(bf16)


def dot(a, b, dims):
    return lax.dot_general(a, b, (dims, ((), ())), preferred_element_type=f32)


def widen(cols, head_size):
    rows, heads = cols.shape
    return jnp.concatenate(
        [jnp.broadcast_to(cols[:, h : h + 1], (rows, head_size)) for h in range(heads)], axis=1
    )


def exchange_kernel(count, src_ref, out_ref, send_sem, recv_sem, own_sem):
    me = lax.axis_index("dp")
    barrier = pltpu.get_barrier_semaphore()

    def greet(step, carry):
        peer = lax.rem(me + step, count)
        pl.semaphore_signal(
            barrier, inc=1, device_id={"dp": peer}, device_id_type=pl.DeviceIdType.MESH
        )
        return carry

    lax.fori_loop(1, count, greet, 0)
    pl.semaphore_wait(barrier, count - 1)

    def copy(step):
        peer = lax.rem(me + step, count)
        return pltpu.make_async_remote_copy(
            src_ref=src_ref.at[peer],
            dst_ref=out_ref.at[me],
            send_sem=send_sem.at[step],
            recv_sem=recv_sem.at[step],
            device_id={"dp": peer},
            device_id_type=pl.DeviceIdType.MESH,
        )

    def start(step, carry):
        copy(step).start()
        return carry

    def finish(step, carry):
        copy(step).wait()
        return carry

    lax.fori_loop(1, count, start, 0)
    mine = pltpu.make_async_copy(src_ref.at[me], out_ref.at[me], own_sem)
    mine.start()
    mine.wait()
    lax.fori_loop(1, count, finish, 0)


def exchange(a, count, collective_id):
    return pl.pallas_call(
        lambda *refs: exchange_kernel(count, *refs),
        out_shape=jax.ShapeDtypeStruct(a.shape, a.dtype),
        in_specs=[pl.BlockSpec(memory_space=pltpu.VMEM)],
        out_specs=pl.BlockSpec(memory_space=pltpu.VMEM),
        scratch_shapes=[
            pltpu.SemaphoreType.DMA((count,)),
            pltpu.SemaphoreType.DMA((count,)),
            pltpu.SemaphoreType.DMA,
        ],
        compiler_params=pltpu.CompilerParams(
            collective_id=collective_id, has_side_effects=True, vmem_limit_bytes=16 << 20
        ),
        cost_estimate=pl.CostEstimate(flops=0, bytes_accessed=12 << 20, transcendentals=0),
        name="exchange",
    )(a)


def prepare_kernel(
    groups, state_size, lags, dt_ref, bias_ref, decay_ref, bc_ref, tail_ref, conv_ref,
    cum_ref, step_ref, score_ref, scoret_ref, cc_ref, act_ref, u8_ref, ext,
):
    rows = dt_ref.shape[0]
    row = lax.broadcasted_iota(jnp.int32, (rows, rows), 0)
    col = lax.broadcasted_iota(jnp.int32, (rows, rows), 1)
    logits = dt_ref[...].astype(f32) + bias_ref[...]
    step = jnp.maximum(logits, 0.0) + jnp.log1p(jnp.exp(-jnp.abs(logits)))
    dec = -step * jnp.exp(decay_ref[...])
    step_ref[...] = step.T
    cum_ref[...] = lax.dot_general(
        dec.T, jnp.where(row <= col, 1.0, 0.0), (((1,), (0,)), ((), ())),
        precision=highest, preferred_element_type=f32,
    )
    ext[0:8, :] = tail_ref[...]
    ext[8:, :] = bc_ref[...].astype(f32)
    conv = conv_ref[...]
    u = conv[0:1] * ext[8 - lags : 8 - lags + rows, :]
    for k in range(1, lags + 1):
        u = u + conv[k : k + 1] * ext[8 - lags + k : 8 - lags + k + rows, :]
    u8_ref[...] = u[:8]
    act = u * (1.0 / (1.0 + jnp.exp(-u)))
    act_ref[...] = act
    for g in range(groups):
        b = act[:, g * state_size : (g + 1) * state_size]
        c = act[:, (groups + g) * state_size : (groups + g + 1) * state_size]
        score = lax.dot_general(
            c, b, (((1,), (1,)), ((), ())), precision=highest, preferred_element_type=f32
        )
        score = jnp.where(row >= col, score, 0.0)
        score_ref[g] = score
        scoret_ref[g] = score.T[:8]
        hi, lo = split(c)
        cc_ref[g, :, :state_size] = hi
        cc_ref[g, :, state_size:] = lo


def within_kernel(
    blocks_per_group, head_size, lags, own, x_ref, cot_ref, tail_ref, conv_ref, cumr_ref,
    delr_ref, wt_ref, wrow_ref, skip_ref, score_ref, scoret_ref, cc_ref, y_ref, dst_ref, dtail_ref, dscore_ref, ext,
):
    j = pl.program_id(0)
    rows = x_ref.shape[0]
    heads = cumr_ref.shape[0]
    state_size = cc_ref.shape[2] // 2
    ext[0:8, :] = tail_ref[...]
    ext[8:, :] = x_ref[...].astype(f32)
    conv = conv_ref[...]
    u = conv[0:1] * ext[8 - lags : 8 - lags + rows, :]
    for k in range(1, lags + 1):
        u = u + conv[k : k + 1] * ext[8 - lags + k : 8 - lags + k + rows, :]
    sig = 1.0 / (1.0 + jnp.exp(-u))
    act = u * sig
    act_hi, act_lo = split(act)
    cumr = cumr_ref[...]
    delr = delr_ref[...]
    cumc = cumr.T
    delc8 = delr.T[:8]
    weight = wt_ref[...]
    wrow = wrow_ref[...]
    score = score_ref[0]
    score_t = scoret_ref[0] * wrow
    cot = cot_ref[...]
    pair = 2 * head_size
    first = lax.broadcasted_iota(jnp.int32, (1, pair), 1) < head_size
    parts, dvals = [], []
    dscore = jnp.zeros((8, rows), f32)
    for p in range(heads // 2):
        lanes = slice(p * pair, (p + 1) * pair)
        lhs, grads, decays = [], [], []
        for h in (2 * p, 2 * p + 1):
            gap = cumc[:, h : h + 1] - cumr[h : h + 1, :]
            mix = jnp.exp(jnp.minimum(gap, 0.0)) * delr[h : h + 1, :] * score
            lhs.extend(split(mix))
            gap8 = cumr[h : h + 1, :] - cumc[:8, h : h + 1]
            decay8 = jnp.exp(jnp.minimum(gap8, 0.0)) * delc8[:, h : h + 1]
            decays.append(decay8)
            mix8 = decay8 * score_t
            hi8 = mix8.astype(bf16).astype(f32)
            grads.extend([hi8, mix8 - hi8])
        wide = dot(
            jnp.concatenate(lhs, axis=0),
            jnp.concatenate([act_hi[:, lanes], act_lo[:, lanes]], axis=1),
            ((1,), (0,)),
        )
        even = wide[:rows, :pair] + wide[:rows, pair:] + wide[rows : 2 * rows, :pair]
        odd = wide[2 * rows : 3 * rows, :pair] + wide[2 * rows : 3 * rows, pair:] + wide[3 * rows :, :pair]
        parts.append(jnp.where(first, even, odd))
        cot_p = cot[:, lanes]
        both = dot(jnp.concatenate(grads, axis=0).astype(bf16), cot_p, ((1,), (0,)))
        dvals.append(jnp.where(first, both[:8] + both[8:16], both[16:24] + both[24:]))
        a8 = act[:8, lanes]
        h8 = a8.astype(bf16).astype(f32)
        l8 = a8 - h8
        zero = jnp.zeros_like(a8)
        picks = jnp.concatenate(
            [jnp.where(first, h8, zero), jnp.where(first, l8, zero),
             jnp.where(first, zero, h8), jnp.where(first, zero, l8)], axis=0,
        ).astype(bf16)
        q = dot(picks, cot_p, ((1,), (1,)))
        dscore = dscore + decays[0] * (q[:8] + q[8:16]) + decays[1] * (q[16:24] + q[24:])
    skip = skip_ref[...]
    y_ref[...] = jnp.concatenate(parts, axis=1) + skip * act
    dscore = dscore * wrow

    @pl.when(lax.rem(j, blocks_per_group) == 0)
    def _():
        dscore_ref[0] = dscore

    @pl.when(lax.rem(j, blocks_per_group) != 0)
    def _():
        dscore_ref[0] += dscore

    cot32 = cot.astype(f32)
    z_hi, z_lo = split(cot32 * widen(jnp.exp(cumc) * weight, head_size))
    cc = cc_ref[0]
    wide = dot(z_hi, cc, ((0,), (0,)))
    dst = wide[:, :state_size] + wide[:, state_size:] + dot(z_lo, cc[:, :state_size], ((0,), (0,)))
    dst_ref[0] = dst.astype(bf16)

    dact = jnp.concatenate(dvals, axis=1) + skip * cot32[:8] * weight[:8]
    u8, s8 = u[:8], sig[:8]
    dtail_ref[...] = dact * (s8 * (1.0 + u8 * (1.0 - s8)))


def carried_kernel(
    blocks_per_group, head_size, own, y_ref, cot_ref, cumr_ref, wt_ref, cc_ref, state_ref, out_ref, dc_ref
):
    j = pl.program_id(0)
    state_size = state_ref.shape[2]
    state = state_ref[0]
    cc = cc_ref[0]
    carried = dot(cc[:, :state_size], state, ((1,), (1,))) + dot(
        cc[:, state_size:], state, ((1,), (1,))
    )
    gains = jnp.exp(cumr_ref[...]).T
    wide = widen(gains, head_size)
    out_ref[...] = (y_ref[...] + wide * carried).astype(bf16)
    z = cot_ref[...][:8].astype(f32) * (wide[:8] * wt_ref[...][:8])
    z_hi, z_lo = split(z)
    dc = dot(z_hi, state, ((1,), (0,))) + dot(z_lo, state, ((1,), (0,)))

    @pl.when(lax.rem(j, blocks_per_group) == 0)
    def _():
        dc_ref[0] = dc

    @pl.when(lax.rem(j, blocks_per_group) != 0)
    def _():
        dc_ref[0] += dc


def local(
    x_input, bc_input, dt_input, out_cotangent, prompt_states, prompt_tails, rewards, lengths,
    owners, conv_weight, decay_log, dt_bias, skip_gain,
):
    device_count = lax.axis_size("dp")
    my_index = lax.axis_index("dp")
    prompt_count, resp_count = owners.shape
    _, block_heads, head_size, state_size = prompt_states.shape
    lags, tail_width = prompt_tails.shape[1:]
    rows, inner = x_input.shape
    heads = dt_input.shape[1]
    group_width = bc_input.shape[1] // 2
    groups = group_width // state_size
    width = block_heads * head_size
    per_group = resp_count // groups
    tail_len = lags * tail_width
    holder_ids = jnp.arange(device_count, dtype=jnp.int32)
    prompt_ids = jnp.arange(prompt_count, dtype=jnp.int32)

    small = jnp.concatenate([prompt_tails.reshape(-1).astype(f32), rewards.astype(f32)])
    small = jnp.pad(small, (0, -small.shape[0] % 1024)).reshape(1, -1, 128)
    small = jnp.broadcast_to(small, (device_count,) + small.shape[1:])
    small = exchange(small, device_count, 1).reshape(device_count, -1)
    chips = device_count // 2
    lanes_of = [[2 * i + c for i in range(chips)] for c in range(2)]
    swap = [(i, i ^ 1) for i in range(device_count)]
    block, small = lax.optimization_barrier((prompt_states.reshape(1, width, state_size), small))
    half = lax.all_to_all(
        jnp.broadcast_to(block, (chips, width, state_size)), "dp", split_axis=0, concat_axis=0,
        axis_index_groups=lanes_of, tiled=True,
    )
    states = jnp.concatenate([half, lax.ppermute(half, "dp", swap)], axis=0)

    matches = owners[:, :, None] == holder_ids[None, None, :]
    held_prompt = jnp.sum(jnp.where(matches, prompt_ids[:, None, None], 0), axis=(0, 1))
    my_prompt = jnp.sum(jnp.where(holder_ids == my_index, held_prompt, 0))
    owner_row = jnp.sum(jnp.where((prompt_ids == my_prompt)[:, None], owners, 0), axis=0)
    core = my_index % 2
    place = jnp.where(owner_row % 2 == core, 0, chips) + owner_row // 2
    pick = (owner_row[:, None] == holder_ids[None, :]).astype(f32)

    member = (held_prompt == my_prompt).astype(f32)
    reward_all = small[:, tail_len]
    mean_value = jnp.sum(member * reward_all) / resp_count
    spread_value = jnp.sum(member * (reward_all - mean_value) ** 2) / resp_count
    advantage = (rewards[0] - mean_value) / jnp.maximum(jnp.sqrt(spread_value), 1.0)
    length = lengths[0]
    alive = (jnp.arange(rows, dtype=jnp.int32) < length).astype(f32)
    weight = (advantage * alive / length.astype(f32))[:, None]

    tails = jnp.dot(pick, small[:, :tail_len], precision=highest)
    tails = tails.reshape(resp_count, lags, tail_width).transpose(1, 0, 2).reshape(lags, -1)

    tail8 = jnp.pad(tails, ((8 - lags, 0), (0, 0)))
    causal = jnp.arange(rows)[:, None] >= jnp.arange(rows)[None, :]
    cumr, delr, scores, scores_t, cc, bc_act, bc_u = pl.pallas_call(
        lambda *refs: prepare_kernel(groups, state_size, lags, *refs),
        out_shape=[
            jax.ShapeDtypeStruct((heads, rows), f32),
            jax.ShapeDtypeStruct((heads, rows), f32),
            jax.ShapeDtypeStruct((groups, rows, rows), f32),
            jax.ShapeDtypeStruct((groups, 8, rows), f32),
            jax.ShapeDtypeStruct((groups, rows, 2 * state_size), bf16),
            jax.ShapeDtypeStruct((rows, 2 * group_width), f32),
            jax.ShapeDtypeStruct((8, 2 * group_width), f32),
        ],
        scratch_shapes=[pltpu.VMEM((rows + 8, 2 * group_width), f32)],
        compiler_params=pltpu.CompilerParams(vmem_limit_bytes=24 << 20),
        name="prepare",
    )(dt_input, dt_bias[None, :], decay_log[None, :], bc_input, tail8[:, inner:], conv_weight[:, inner:])
    b_proj = bc_act[:, :group_width].reshape(rows, groups, state_size)
    c_proj = bc_act[:, group_width:].reshape(rows, groups, state_size)
    skip = jnp.repeat(skip_gain, head_size)[None, :]
    taps = conv_weight.shape[0]

    wide_spec = pl.BlockSpec((rows, width), lambda j, own: (0, j))
    row_spec = pl.BlockSpec((block_heads, rows), lambda j, own: (j, 0))
    wt_spec = pl.BlockSpec((rows, 1), lambda j, own: (0, 0))
    cc_spec = pl.BlockSpec((1, rows, 2 * state_size), lambda j, own: (j // per_group, 0, 0))
    slot_spec = pl.BlockSpec((1, width, state_size), lambda j, own: (own[j], 0, 0))
    eight = pl.BlockSpec((8, width), lambda j, own: (0, j))

    y_part, dstate, du_x, dscore = pl.pallas_call(
        lambda *refs: within_kernel(per_group, head_size, lags, *refs),
        grid_spec=pltpu.PrefetchScalarGridSpec(
            num_scalar_prefetch=1,
            grid=(resp_count,),
            in_specs=[
                wide_spec,
                wide_spec,
                eight,
                pl.BlockSpec((taps, width), lambda j, own: (0, j)),
                row_spec,
                row_spec,
                wt_spec,
                pl.BlockSpec((1, rows), lambda j, own: (0, 0)),
                pl.BlockSpec((1, width), lambda j, own: (0, j)),
                pl.BlockSpec((1, rows, rows), lambda j, own: (j // per_group, 0, 0)),
                pl.BlockSpec((1, 8, rows), lambda j, own: (j // per_group, 0, 0)),
                cc_spec,
            ],
            out_specs=[
                wide_spec,
                slot_spec,
                eight,
                pl.BlockSpec((1, 8, rows), lambda j, own: (j // per_group, 0, 0)),
            ],
            scratch_shapes=[pltpu.VMEM((rows + 8, width), f32)],
        ),
        out_shape=[
            jax.ShapeDtypeStruct((rows, inner), f32),
            jax.ShapeDtypeStruct((device_count, width, state_size), bf16),
            jax.ShapeDtypeStruct((8, inner), f32),
            jax.ShapeDtypeStruct((groups, 8, rows), f32),
        ],
        compiler_params=pltpu.CompilerParams(vmem_limit_bytes=24 << 20),
        cost_estimate=pl.CostEstimate(flops=3 << 30, bytes_accessed=12 << 20, transcendentals=4 << 20),
        name="within",
    )(place, x_input, out_cotangent, tail8, conv_weight, cumr, delr, weight, weight.T, skip, scores, scores_t, cc)

    if prompt_count > 1:
        used = jnp.any(place[:, None] == holder_ids[None, :], axis=0)
        dstate = jnp.where(used[:, None, None], dstate, jnp.zeros_like(dstate))
    other = lax.ppermute(dstate[chips:], "dp", swap)
    chip_sums = (dstate[:chips].astype(f32) + other.astype(f32)).astype(bf16)
    got = lax.all_to_all(
        chip_sums, "dp", split_axis=0, concat_axis=0, axis_index_groups=lanes_of, tiled=True
    )

    layer_out, dc_state = pl.pallas_call(
        lambda *refs: carried_kernel(per_group, head_size, *refs),
        grid_spec=pltpu.PrefetchScalarGridSpec(
            num_scalar_prefetch=1,
            grid=(resp_count,),
            in_specs=[wide_spec, pl.BlockSpec((16, width), lambda j, own: (0, j)), row_spec, wt_spec, cc_spec, slot_spec],
            out_specs=[
                wide_spec,
                pl.BlockSpec((1, 8, state_size), lambda j, own: (j // per_group, 0, 0)),
            ],
        ),
        out_shape=[
            jax.ShapeDtypeStruct((rows, inner), bf16),
            jax.ShapeDtypeStruct((groups, 8, state_size), f32),
        ],
        compiler_params=pltpu.CompilerParams(vmem_limit_bytes=24 << 20),
        cost_estimate=pl.CostEstimate(flops=1 << 30, bytes_accessed=9 << 20, transcendentals=1 << 17),
        name="carried",
    )(place, y_part, out_cotangent, cumr, weight, cc, states)

    keep = jnp.where(causal[:, :8].T[None], dscore, 0.0)
    db = jnp.einsum("gst,tgn->sgn", keep, c_proj, precision=highest).reshape(8, group_width)
    dc = jnp.einsum("gst,sgn->tgn", keep[:, :, :8], b_proj[:8], precision=highest)
    dc = (dc + dc_state.transpose(1, 0, 2)).reshape(8, group_width)
    sig = jax.nn.sigmoid(bc_u[:8])
    du_bc = jnp.concatenate([db, dc], axis=1) * (sig * (1.0 + bc_u[:8] * (1.0 - sig)))
    du = jnp.concatenate([du_x, du_bc], axis=1)
    dtail = jnp.stack(
        [sum(conv_weight[m - t] * du[t] for t in range(m + 1)) for m in range(lags)]
    ).astype(bf16)
    tail_blocks = dtail.reshape(lags, resp_count, tail_width).transpose(1, 0, 2)
    tail_blocks = tail_blocks.reshape(resp_count, tail_len)
    tail_send = jnp.dot(pick.T.astype(bf16), tail_blocks, preferred_element_type=f32).astype(bf16)
    tail_send = jnp.pad(tail_send, ((0, 0), (0, -tail_len % 2048))).reshape(device_count, -1, 128)
    got_tail = exchange(tail_send, device_count, 2).reshape(device_count, -1)[:, :tail_len]

    state_grad = jnp.sum(got.astype(f32), axis=0)
    state_grad = state_grad.reshape(1, block_heads, head_size, state_size)
    tail_grad = jnp.sum(got_tail.astype(f32), axis=0).reshape(1, lags, tail_width)
    return layer_out, state_grad, tail_grad


def solution(mesh):
    in_specs = (
        P(("groups", "dp"), None),
        P(("groups", "dp"), None),
        P(("groups", "dp"), None),
        P(("groups", "dp"), None),
        P(("groups", "dp"), None, None, None),
        P(("groups", "dp"), None, None),
        P(("groups", "dp")),
        P(("groups", "dp")),
        P("groups", None),
        P(),
        P(),
        P(),
        P(),
    )
    out_specs = (
        P(("groups", "dp"), None),
        P(("groups", "dp"), None, None, None),
        P(("groups", "dp"), None, None),
    )
    return jax.shard_map(local, mesh=mesh, in_specs=in_specs, out_specs=out_specs, check_vma=False)
```

```python
import jax
import jax.numpy as jnp
from jax import lax
from jax.experimental import pallas as pl
from jax.experimental.pallas import tpu as pltpu
from jax.sharding import PartitionSpec as P

highest = lax.Precision.HIGHEST
f32 = jnp.float32
bf16 = jnp.bfloat16


def split(a):
    hi = a.astype(bf16)
    return hi, (a - hi.astype(f32)).astype(bf16)


def dot(a, b, dims):
    return lax.dot_general(a, b, (dims, ((), ())), preferred_element_type=f32)


def widen(cols, head_size):
    rows, heads = cols.shape
    first = lax.broadcasted_iota(jnp.int32, (rows, 2 * head_size), 1) < head_size
    return jnp.concatenate(
        [jnp.where(first, cols[:, h : h + 1], cols[:, h + 1 : h + 2]) for h in range(0, heads, 2)],
        axis=1,
    )


def exchange_kernel(count, src_ref, out_ref, send_sem, recv_sem, own_sem):
    me = lax.axis_index("dp")
    barrier = pltpu.get_barrier_semaphore()

    def greet(step, carry):
        peer = lax.rem(me + step, count)
        pl.semaphore_signal(
            barrier, inc=1, device_id={"dp": peer}, device_id_type=pl.DeviceIdType.MESH
        )
        return carry

    lax.fori_loop(1, count, greet, 0)
    pl.semaphore_wait(barrier, count - 1)

    def copy(step):
        peer = lax.rem(me + step, count)
        return pltpu.make_async_remote_copy(
            src_ref=src_ref.at[peer],
            dst_ref=out_ref.at[me],
            send_sem=send_sem.at[step],
            recv_sem=recv_sem.at[step],
            device_id={"dp": peer},
            device_id_type=pl.DeviceIdType.MESH,
        )

    def start(step, carry):
        copy(step).start()
        return carry

    def finish(step, carry):
        copy(step).wait()
        return carry

    lax.fori_loop(1, count, start, 0)
    mine = pltpu.make_async_copy(src_ref.at[me], out_ref.at[me], own_sem)
    mine.start()
    mine.wait()
    lax.fori_loop(1, count, finish, 0)


def exchange(a, count, collective_id):
    return pl.pallas_call(
        lambda *refs: exchange_kernel(count, *refs),
        out_shape=jax.ShapeDtypeStruct(a.shape, a.dtype),
        in_specs=[pl.BlockSpec(memory_space=pltpu.VMEM)],
        out_specs=pl.BlockSpec(memory_space=pltpu.VMEM),
        scratch_shapes=[
            pltpu.SemaphoreType.DMA((count,)),
            pltpu.SemaphoreType.DMA((count,)),
            pltpu.SemaphoreType.DMA,
        ],
        compiler_params=pltpu.CompilerParams(
            collective_id=collective_id, has_side_effects=True, vmem_limit_bytes=16 << 20
        ),
        cost_estimate=pl.CostEstimate(flops=0, bytes_accessed=12 << 20, transcendentals=0),
        name="exchange",
    )(a)


def prepare_kernel(
    groups, state_size, lags, dt_ref, bias_ref, decay_ref, bc_ref, tail_ref, conv_ref,
    cum_ref, step_ref, score_ref, scoret_ref, cc_ref, act_ref, u8_ref, ext,
):
    rows = dt_ref.shape[0]
    row = lax.broadcasted_iota(jnp.int32, (rows, rows), 0)
    col = lax.broadcasted_iota(jnp.int32, (rows, rows), 1)
    logits = dt_ref[...].astype(f32) + bias_ref[...]
    step = jnp.maximum(logits, 0.0) + jnp.log1p(jnp.exp(-jnp.abs(logits)))
    dec = -step * jnp.exp(decay_ref[...])
    step_ref[...] = step.T
    cum_ref[...] = lax.dot_general(
        dec.T, jnp.where(row <= col, 1.0, 0.0), (((1,), (0,)), ((), ())),
        precision=highest, preferred_element_type=f32,
    )
    ext[0:8, :] = tail_ref[...]
    ext[8:, :] = bc_ref[...].astype(f32)
    conv = conv_ref[...]
    u = conv[0:1] * ext[8 - lags : 8 - lags + rows, :]
    for k in range(1, lags + 1):
        u = u + conv[k : k + 1] * ext[8 - lags + k : 8 - lags + k + rows, :]
    u8_ref[...] = u[:8]
    act = u * (1.0 / (1.0 + jnp.exp(-u)))
    act_ref[...] = act
    for g in range(groups):
        b = act[:, g * state_size : (g + 1) * state_size]
        c = act[:, (groups + g) * state_size : (groups + g + 1) * state_size]
        score = lax.dot_general(
            c, b, (((1,), (1,)), ((), ())), precision=highest, preferred_element_type=f32
        )
        score = jnp.where(row >= col, score, 0.0)
        score_ref[g] = score
        scoret_ref[g] = score.T[:8]
        hi, lo = split(c)
        cc_ref[g, :, :state_size] = hi
        cc_ref[g, :, state_size:] = lo


def within_kernel(
    blocks_per_group, head_size, lags, own, x_ref, cot_ref, tail_ref, conv_ref, cumr_ref,
    delr_ref, wt_ref, wrow_ref, skip_ref, score_ref, scoret_ref, cc_ref, y_ref, dst_ref, dtail_ref, dscore_ref, ext,
):
    j = pl.program_id(0)
    rows = x_ref.shape[0]
    heads = cumr_ref.shape[0]
    state_size = cc_ref.shape[2] // 2
    ext[0:8, :] = tail_ref[...]
    ext[8:, :] = x_ref[...].astype(f32)
    conv = conv_ref[...]
    u = conv[0:1] * ext[8 - lags : 8 - lags + rows, :]
    for k in range(1, lags + 1):
        u = u + conv[k : k + 1] * ext[8 - lags + k : 8 - lags + k + rows, :]
    sig = 1.0 / (1.0 + jnp.exp(-u))
    act = u * sig
    act_hi, act_lo = split(act)
    cumr = cumr_ref[...]
    delr = delr_ref[...]
    cumc = cumr.T
    delc8 = delr.T[:8]
    weight = wt_ref[...]
    wrow = wrow_ref[...]
    score = score_ref[0]
    score_t = scoret_ref[0] * wrow
    cot = cot_ref[...]
    pair = 2 * head_size
    first = lax.broadcasted_iota(jnp.int32, (1, pair), 1) < head_size
    parts, dvals = [], []
    dscore = jnp.zeros((8, rows), f32)
    for p in range(heads // 2):
        lanes = slice(p * pair, (p + 1) * pair)
        lhs, grads, decays = [], [], []
        for h in (2 * p, 2 * p + 1):
            gap = cumc[:, h : h + 1] - cumr[h : h + 1, :]
            mix = jnp.exp(jnp.minimum(gap, 0.0)) * delr[h : h + 1, :] * score
            lhs.extend(split(mix))
            gap8 = cumr[h : h + 1, :] - cumc[:8, h : h + 1]
            decay8 = jnp.exp(jnp.minimum(gap8, 0.0)) * delc8[:, h : h + 1]
            decays.append(decay8)
            mix8 = decay8 * score_t
            hi8 = mix8.astype(bf16).astype(f32)
            grads.extend([hi8, mix8 - hi8])
        wide = dot(
            jnp.concatenate(lhs, axis=0),
            jnp.concatenate([act_hi[:, lanes], act_lo[:, lanes]], axis=1),
            ((1,), (0,)),
        )
        even = wide[:rows, :pair] + wide[:rows, pair:] + wide[rows : 2 * rows, :pair]
        odd = wide[2 * rows : 3 * rows, :pair] + wide[2 * rows : 3 * rows, pair:] + wide[3 * rows :, :pair]
        parts.append(jnp.where(first, even, odd))
        cot_p = cot[:, lanes]
        both = dot(jnp.concatenate(grads, axis=0).astype(bf16), cot_p, ((1,), (0,)))
        dvals.append(jnp.where(first, both[:8] + both[8:16], both[16:24] + both[24:]))
        a8 = act[:8, lanes]
        h8 = a8.astype(bf16).astype(f32)
        l8 = a8 - h8
        zero = jnp.zeros_like(a8)
        picks = jnp.concatenate(
            [jnp.where(first, h8, zero), jnp.where(first, l8, zero),
             jnp.where(first, zero, h8), jnp.where(first, zero, l8)], axis=0,
        ).astype(bf16)
        q = dot(picks, cot_p, ((1,), (1,)))
        dscore = dscore + decays[0] * (q[:8] + q[8:16]) + decays[1] * (q[16:24] + q[24:])
    skip = skip_ref[...]
    y_ref[...] = jnp.concatenate(parts, axis=1) + skip * act
    dscore = dscore * wrow

    @pl.when(lax.rem(j, blocks_per_group) == 0)
    def _():
        dscore_ref[0] = dscore

    @pl.when(lax.rem(j, blocks_per_group) != 0)
    def _():
        dscore_ref[0] += dscore

    cot32 = cot.astype(f32)
    z_hi, z_lo = split(cot32 * widen(jnp.exp(cumc) * weight, head_size))
    cc = cc_ref[0]
    wide = dot(z_hi, cc, ((0,), (0,)))
    dst = wide[:, :state_size] + wide[:, state_size:] + dot(z_lo, cc[:, :state_size], ((0,), (0,)))
    dst_ref[0] = dst.astype(bf16)

    dact = jnp.concatenate(dvals, axis=1) + skip * cot32[:8] * weight[:8]
    u8, s8 = u[:8], sig[:8]
    dtail_ref[...] = dact * (s8 * (1.0 + u8 * (1.0 - s8)))


def carried_kernel(
    blocks_per_group, head_size, own, y_ref, cot_ref, cumr_ref, wt_ref, cc_ref, state_ref, out_ref, dc_ref
):
    j = pl.program_id(0)
    state_size = state_ref.shape[2]
    state = state_ref[0]
    cc = cc_ref[0]
    carried = dot(cc[:, :state_size], state, ((1,), (1,))) + dot(
        cc[:, state_size:], state, ((1,), (1,))
    )
    gains = jnp.exp(cumr_ref[...]).T
    wide = widen(gains, head_size)
    out_ref[...] = (y_ref[...] + wide * carried).astype(bf16)
    z = cot_ref[...][:8].astype(f32) * (wide[:8] * wt_ref[...][:8])
    z_hi, z_lo = split(z)
    dc = dot(z_hi, state, ((1,), (0,))) + dot(z_lo, state, ((1,), (0,)))

    @pl.when(lax.rem(j, blocks_per_group) == 0)
    def _():
        dc_ref[0] = dc

    @pl.when(lax.rem(j, blocks_per_group) != 0)
    def _():
        dc_ref[0] += dc


def local(
    x_input, bc_input, dt_input, out_cotangent, prompt_states, prompt_tails, rewards, lengths,
    owners, conv_weight, decay_log, dt_bias, skip_gain,
):
    device_count = lax.axis_size("dp")
    my_index = lax.axis_index("dp")
    prompt_count, resp_count = owners.shape
    _, block_heads, head_size, state_size = prompt_states.shape
    lags, tail_width = prompt_tails.shape[1:]
    rows, inner = x_input.shape
    heads = dt_input.shape[1]
    group_width = bc_input.shape[1] // 2
    groups = group_width // state_size
    width = block_heads * head_size
    per_group = resp_count // groups
    tail_len = lags * tail_width
    holder_ids = jnp.arange(device_count, dtype=jnp.int32)
    prompt_ids = jnp.arange(prompt_count, dtype=jnp.int32)

    small = jnp.concatenate([prompt_tails.reshape(-1).astype(f32), rewards.astype(f32)])
    small = jnp.pad(small, (0, -small.shape[0] % 1024)).reshape(1, -1, 128)
    small = jnp.broadcast_to(small, (device_count,) + small.shape[1:])
    small = exchange(small, device_count, 1).reshape(device_count, -1)
    chips = device_count // 2
    lanes_of = [[2 * i + c for i in range(chips)] for c in range(2)]
    swap = [(i, i ^ 1) for i in range(device_count)]
    block, small = lax.optimization_barrier((prompt_states.reshape(1, width, state_size), small))
    half = lax.all_to_all(
        jnp.broadcast_to(block, (chips, width, state_size)), "dp", split_axis=0, concat_axis=0,
        axis_index_groups=lanes_of, tiled=True,
    )
    states = jnp.concatenate([half, lax.ppermute(half, "dp", swap)], axis=0)

    matches = owners[:, :, None] == holder_ids[None, None, :]
    held_prompt = jnp.sum(jnp.where(matches, prompt_ids[:, None, None], 0), axis=(0, 1))
    my_prompt = jnp.sum(jnp.where(holder_ids == my_index, held_prompt, 0))
    owner_row = jnp.sum(jnp.where((prompt_ids == my_prompt)[:, None], owners, 0), axis=0)
    core = my_index % 2
    place = jnp.where(owner_row % 2 == core, 0, chips) + owner_row // 2
    pick = (owner_row[:, None] == holder_ids[None, :]).astype(f32)

    member = (held_prompt == my_prompt).astype(f32)
    reward_all = small[:, tail_len]
    mean_value = jnp.sum(member * reward_all) / resp_count
    spread_value = jnp.sum(member * (reward_all - mean_value) ** 2) / resp_count
    advantage = (rewards[0] - mean_value) / jnp.maximum(jnp.sqrt(spread_value), 1.0)
    length = lengths[0]
    alive = (jnp.arange(rows, dtype=jnp.int32) < length).astype(f32)
    weight = (advantage * alive / length.astype(f32))[:, None]

    tails = jnp.dot(pick, small[:, :tail_len], precision=highest)
    tails = tails.reshape(resp_count, lags, tail_width).transpose(1, 0, 2).reshape(lags, -1)

    tail8 = jnp.pad(tails, ((8 - lags, 0), (0, 0)))
    causal = jnp.arange(rows)[:, None] >= jnp.arange(rows)[None, :]
    cumr, delr, scores, scores_t, cc, bc_act, bc_u = pl.pallas_call(
        lambda *refs: prepare_kernel(groups, state_size, lags, *refs),
        out_shape=[
            jax.ShapeDtypeStruct((heads, rows), f32),
            jax.ShapeDtypeStruct((heads, rows), f32),
            jax.ShapeDtypeStruct((groups, rows, rows), f32),
            jax.ShapeDtypeStruct((groups, 8, rows), f32),
            jax.ShapeDtypeStruct((groups, rows, 2 * state_size), bf16),
            jax.ShapeDtypeStruct((rows, 2 * group_width), f32),
            jax.ShapeDtypeStruct((8, 2 * group_width), f32),
        ],
        scratch_shapes=[pltpu.VMEM((rows + 8, 2 * group_width), f32)],
        compiler_params=pltpu.CompilerParams(vmem_limit_bytes=24 << 20),
        name="prepare",
    )(dt_input, dt_bias[None, :], decay_log[None, :], bc_input, tail8[:, inner:], conv_weight[:, inner:])
    b_proj = bc_act[:, :group_width].reshape(rows, groups, state_size)
    c_proj = bc_act[:, group_width:].reshape(rows, groups, state_size)
    skip = jnp.repeat(skip_gain, head_size)[None, :]
    taps = conv_weight.shape[0]

    wide_spec = pl.BlockSpec((rows, width), lambda j, own: (0, j))
    row_spec = pl.BlockSpec((block_heads, rows), lambda j, own: (j, 0))
    wt_spec = pl.BlockSpec((rows, 1), lambda j, own: (0, 0))
    cc_spec = pl.BlockSpec((1, rows, 2 * state_size), lambda j, own: (j // per_group, 0, 0))
    slot_spec = pl.BlockSpec((1, width, state_size), lambda j, own: (own[j], 0, 0))
    eight = pl.BlockSpec((8, width), lambda j, own: (0, j))

    y_part, dstate, du_x, dscore = pl.pallas_call(
        lambda *refs: within_kernel(per_group, head_size, lags, *refs),
        grid_spec=pltpu.PrefetchScalarGridSpec(
            num_scalar_prefetch=1,
            grid=(resp_count,),
            in_specs=[
                wide_spec,
                wide_spec,
                eight,
                pl.BlockSpec((taps, width), lambda j, own: (0, j)),
                row_spec,
                row_spec,
                wt_spec,
                pl.BlockSpec((1, rows), lambda j, own: (0, 0)),
                pl.BlockSpec((1, width), lambda j, own: (0, j)),
                pl.BlockSpec((1, rows, rows), lambda j, own: (j // per_group, 0, 0)),
                pl.BlockSpec((1, 8, rows), lambda j, own: (j // per_group, 0, 0)),
                cc_spec,
            ],
            out_specs=[
                wide_spec,
                slot_spec,
                eight,
                pl.BlockSpec((1, 8, rows), lambda j, own: (j // per_group, 0, 0)),
            ],
            scratch_shapes=[pltpu.VMEM((rows + 8, width), f32)],
        ),
        out_shape=[
            jax.ShapeDtypeStruct((rows, inner), f32),
            jax.ShapeDtypeStruct((device_count, width, state_size), bf16),
            jax.ShapeDtypeStruct((8, inner), f32),
            jax.ShapeDtypeStruct((groups, 8, rows), f32),
        ],
        compiler_params=pltpu.CompilerParams(vmem_limit_bytes=24 << 20),
        cost_estimate=pl.CostEstimate(flops=3 << 30, bytes_accessed=12 << 20, transcendentals=4 << 20),
        name="within",
    )(place, x_input, out_cotangent, tail8, conv_weight, cumr, delr, weight, weight.T, skip, scores, scores_t, cc)

    if prompt_count > 1:
        used = jnp.any(place[:, None] == holder_ids[None, :], axis=0)
        dstate = jnp.where(used[:, None, None], dstate, jnp.zeros_like(dstate))
    other = lax.ppermute(dstate[chips:], "dp", swap)
    chip_sums = (dstate[:chips].astype(f32) + other.astype(f32)).astype(bf16)
    got = lax.all_to_all(
        chip_sums, "dp", split_axis=0, concat_axis=0, axis_index_groups=lanes_of, tiled=True
    )

    layer_out, dc_state = pl.pallas_call(
        lambda *refs: carried_kernel(per_group, head_size, *refs),
        grid_spec=pltpu.PrefetchScalarGridSpec(
            num_scalar_prefetch=1,
            grid=(resp_count,),
            in_specs=[wide_spec, pl.BlockSpec((16, width), lambda j, own: (0, j)), row_spec, wt_spec, cc_spec, slot_spec],
            out_specs=[
                wide_spec,
                pl.BlockSpec((1, 8, state_size), lambda j, own: (j // per_group, 0, 0)),
            ],
        ),
        out_shape=[
            jax.ShapeDtypeStruct((rows, inner), bf16),
            jax.ShapeDtypeStruct((groups, 8, state_size), f32),
        ],
        compiler_params=pltpu.CompilerParams(vmem_limit_bytes=24 << 20),
        cost_estimate=pl.CostEstimate(flops=1 << 30, bytes_accessed=9 << 20, transcendentals=1 << 17),
        name="carried",
    )(place, y_part, out_cotangent, cumr, weight, cc, states)

    keep = jnp.where(causal[:, :8].T[None], dscore, 0.0)
    db = jnp.einsum("gst,tgn->sgn", keep, c_proj, precision=highest).reshape(8, group_width)
    dc = jnp.einsum("gst,sgn->tgn", keep[:, :, :8], b_proj[:8], precision=highest)
    dc = (dc + dc_state.transpose(1, 0, 2)).reshape(8, group_width)
    sig = jax.nn.sigmoid(bc_u[:8])
    du_bc = jnp.concatenate([db, dc], axis=1) * (sig * (1.0 + bc_u[:8] * (1.0 - sig)))
    du = jnp.concatenate([du_x, du_bc], axis=1)
    dtail = jnp.stack(
        [sum(conv_weight[m - t] * du[t] for t in range(m + 1)) for m in range(lags)]
    ).astype(bf16)
    tail_blocks = dtail.reshape(lags, resp_count, tail_width).transpose(1, 0, 2)
    tail_blocks = tail_blocks.reshape(resp_count, tail_len)
    tail_send = jnp.dot(pick.T.astype(bf16), tail_blocks, preferred_element_type=f32).astype(bf16)
    tail_send = jnp.pad(tail_send, ((0, 0), (0, -tail_len % 2048))).reshape(device_count, -1, 128)
    got_tail = exchange(tail_send, device_count, 2).reshape(device_count, -1)[:, :tail_len]

    state_grad = jnp.sum(got.astype(f32), axis=0)
    state_grad = state_grad.reshape(1, block_heads, head_size, state_size)
    tail_grad = jnp.sum(got_tail.astype(f32), axis=0).reshape(1, lags, tail_width)
    return layer_out, state_grad, tail_grad


def solution(mesh):
    in_specs = (
        P(("groups", "dp"), None),
        P(("groups", "dp"), None),
        P(("groups", "dp"), None),
        P(("groups", "dp"), None),
        P(("groups", "dp"), None, None, None),
        P(("groups", "dp"), None, None),
        P(("groups", "dp")),
        P(("groups", "dp")),
        P("groups", None),
        P(),
        P(),
        P(),
        P(),
    )
    out_specs = (
        P(("groups", "dp"), None),
        P(("groups", "dp"), None, None, None),
        P(("groups", "dp"), None, None),
    )
    return jax.shard_map(local, mesh=mesh, in_specs=in_specs, out_specs=out_specs, check_vma=False)
```
